256 devices in a mesh: mem: 8 (over y, z_lo), gx: 8 (over x, core), gy: 4 (over z_hi).
Axes of the slice: x: 4, y: 4, z: 8 (z_hi: 4, z_lo: 2; z = z_hi * 2 + z_lo), core: 2. Of those that a mesh axis runs over, the one named last changes fastest.
Arguments:
- background_samples: float32 [256, 256, 1024], P('mem', 'gx', 'gy'), may hold values from -6 to 6
- measured_space_anomalies: float32 [256, 8, 4, 8192], P('mem', 'gx', 'gy'), may hold values from -32 to 32
- innovation_vector: float32 [8, 4, 8, 1024], P('gx', 'gy', 'mem'), may hold values from -6 to 6
- error_spread_squared: float32 [8, 4, 8, 1024], P('gx', 'gy', 'mem'), may hold values from 0.25 to 4
- measured_nearest_anchor: int32 [8, 4, 8, 1024], P('gx', 'gy', 'mem'), may hold values from 0 to 3
- active_measurement_tally: int32 [8, 4, 8], P('gx', 'gy', 'mem'), may hold values from 256 to 1024, as said below
Outputs:
- updated_sample_matrix: float32 [256, 256, 1024], P('mem', 'gx', 'gy')
The draws below stay inside these ranges and needn't reach their ends.
Inputs may be any that keep to these rules, and one draw needn't show every extreme that they name: `active_measurement_tally`: some band has all 1024 slots live and some band only 256.
All inputs are finite; a program needn't handle non-finite values.
Results may differ from the reference program's by a relative error of at most 0.0003.
Values sent between devices are 32-bit elements; how exact they have to be, the bound alone decides.
A program may use at most 128 MiB of HBM per device.

```python
import math
import jax
import jax.numpy as jnp
from jax import lax

MEMBERSHIP_TOTAL = 256
CGX = 4
NS_STEPS = 12
CB = 32
OBS_DEV = 1024
TX = 8
TY = 4
BANDS = 8
NCX = 32
CROWS = 32
LONGITUDE_CELLS = 256
LATITUDE_CELLS = 1024


def draw_active_measurement_tally(key, part):
    cells_total = TX * TY * BANDS
    key_counts, key_full, key_offset = jax.random.split(key, 3)
    counts = jax.random.randint(key_counts, (cells_total,), OBS_DEV // 4, OBS_DEV + 1)
    fullest = jax.random.randint(key_full, (), 0, cells_total)
    offset = jax.random.randint(key_offset, (), 1, cells_total)
    counts = counts.at[fullest].set(OBS_DEV)
    counts = counts.at[(fullest + offset) % cells_total].set(OBS_DEV // 4)
    return counts.reshape(TX, TY, BANDS).astype(jnp.int32)


def draw_measured_space_anomalies(key, part):
    key_noise, key_members, key_slots = jax.random.split(jax.random.fold_in(key, 7), 3)
    mode_count = 2
    jitter = jnp.clip(jax.random.normal(key_noise, (MEMBERSHIP_TOTAL, TX, TY, BANDS, OBS_DEV), jnp.float32), -4.0, 4.0)
    strength = jnp.full((mode_count, 1, TX, TY, BANDS), 4.0, jnp.float32)
    member_pattern = jax.random.uniform(key_members, (mode_count, MEMBERSHIP_TOTAL, TX, TY, BANDS), jnp.float32, -1.7, 1.7) * strength
    slot_pattern = jax.random.uniform(key_slots, (mode_count, TX, TY, BANDS, OBS_DEV), jnp.float32, -1.7, 1.7)
    common = jnp.einsum('rkxyb,rxybo->kxybo', member_pattern, slot_pattern, precision=lax.Precision.HIGHEST)
    combined = jnp.clip(jitter + common, -32.0, 32.0)
    return combined.reshape(MEMBERSHIP_TOTAL, TX, TY, BANDS * OBS_DEV).astype(jnp.float32)


def with_ends(values, own_key, smallest, high):
    longest = values.shape.index(max(values.shape))
    spots = []
    for shift in (0, 1):
        where = [jax.random.randint(jax.random.fold_in(own_key, axis), (), 0, length) for axis, length in enumerate(values.shape)]
        where[longest] = (where[longest] + shift) % values.shape[longest]
        spots.append(tuple(where))
    return values.at[spots[0]].set(smallest).at[spots[1]].set(high)


def block_levels(rng, shape, shards, smallest, largest):
    factor_of = 1.0
    for position, shards_of in shards:
        heights = jax.random.uniform(jax.random.fold_in(jax.random.fold_in(rng, 6), position), (shards_of,), jnp.float32, smallest / len(shards), largest / len(shards))
        factor_of = factor_of * jnp.repeat(jnp.exp(heights), shape[position] // shards_of).reshape((-1,) + (1,) * (len(shape) - 1 - position))
    return factor_of


def normal_values(stream_key, shape, scale, most, cuts=(), kind=jnp.bfloat16):
    array = jax.random.normal(stream_key, shape, jnp.float32) * scale
    if len(cuts) > 0:
        array = block_levels(stream_key, shape, cuts, -0.22, 0.18) * array
    return jnp.clip(array, min=-most, max=most).astype(kind)


def setup_inputs(seed: int = 0) -> dict:
    splits = jax.random.split(jax.random.key(seed), 7)
    return {
        "background_samples": normal_values(splits[0], (MEMBERSHIP_TOTAL, LONGITUDE_CELLS, LATITUDE_CELLS), 1.0, 6.0, ((0, 8), (1, 8), (2, 4)), jnp.float32),
        "measured_space_anomalies": draw_measured_space_anomalies(jax.random.fold_in(splits[6], 71), 0),
        "innovation_vector": normal_values(splits[2], (TX, TY, BANDS, OBS_DEV), 1.0, 6.0, ((0, 8), (1, 4), (2, 8)), jnp.float32),
        "error_spread_squared": jnp.clip(jnp.exp(math.log(4.0) - 2.7725887 * jax.random.uniform(splits[3], (TX, TY, BANDS, OBS_DEV), jnp.float32) ** block_levels(splits[3], (TX, TY, BANDS, OBS_DEV), ((0, 8), (1, 4), (2, 8)), -0.2, 0.2)), 0.25, 4.0),
        "measured_nearest_anchor": with_ends(jax.random.randint(splits[4], (TX, TY, BANDS, OBS_DEV), 0, CGX), jax.random.fold_in(splits[4], 1), 0, CGX - 1).astype(jnp.int32),
        "active_measurement_tally": draw_active_measurement_tally(jax.random.fold_in(splits[6], 71), 0),
    }


precise = lax.Precision.HIGHEST

def transforms_block(obs_block, departure, variance, assign, live_count):
    realization_indices = obs_block.shape[0]
    slots = obs_block.shape[1]
    live_mask = (jnp.arange(slots, dtype=jnp.int32) < live_count).astype(jnp.float32)
    points = jnp.arange(CGX, dtype=jnp.int32)
    distance = (assign[None, :] - points[:, None]).astype(jnp.float32)
    weights = jnp.exp(-0.5 * distance * distance) * live_mask[None, :] / variance[None, :]
    scaled = obs_block[None, :, :] * weights[:, None, :]
    identity = jnp.eye(realization_indices, dtype=jnp.float32)
    covariance = jnp.einsum('pko,jo->pkj', scaled, obs_block, precision=precise) + (realization_indices - 1.0) * identity
    right_side = jnp.einsum('pko,o->pk', scaled, departure, precision=precise)
    frob_norm = jnp.sqrt(lax.optimization_barrier(jnp.sum(covariance * covariance, axis=(1, 2))))
    square_root = covariance / frob_norm[:, None, None]
    inverse = jnp.broadcast_to(identity, covariance.shape)
    for iteration in range(NS_STEPS):
        middle = 1.5 * identity - 0.5 * jnp.einsum('pij,pjk->pik', inverse, square_root, precision=precise)
        square_root = jnp.einsum('pij,pjk->pik', square_root, middle, precision=precise)
        inverse = jnp.einsum('pij,pjk->pik', middle, inverse, precision=precise)
    posterior = jnp.einsum('pij,pjk->pik', inverse, inverse, precision=precise) / frob_norm[:, None, None]
    mean_weights = jnp.einsum('pkj,pj->pk', posterior, right_side, precision=precise)
    return jnp.sqrt(realization_indices - 1.0) * inverse / jnp.sqrt(frob_norm)[:, None, None] + mean_weights[:, :, None]

def tent_x(spacing):
    steps = jnp.arange(2 * spacing, dtype=jnp.float32)
    return 1.0 - jnp.abs(2.0 * steps + 1.0 - 2.0 * spacing) / (2.0 * spacing)

def tent_y(height):
    rows_here = jnp.arange(height, dtype=jnp.float32)
    middle = height // 2
    tent_below = jnp.where(rows_here < middle, (2.0 * middle - 2.0 * rows_here - 1.0) / (2.0 * height), 0.0)
    tent_above = jnp.where(rows_here >= middle, (2.0 * rows_here + 1.0 - 2.0 * middle) / (2.0 * height), 0.0)
    return (tent_below, 1.0 - tent_below - tent_above, tent_above)

def band_delta(transforms, sample_departure_matrix, band_index):
    coarse_cols = transforms.shape[0]
    rows_total = transforms.shape[1]
    realization_indices = sample_departure_matrix.shape[0]
    spacing = sample_departure_matrix.shape[1] // coarse_cols
    band_strip = lax.dynamic_slice_in_dim(sample_departure_matrix, band_index * CB, CB, axis=2)
    rolled = jnp.roll(band_strip, spacing // 2, axis=1).reshape(realization_indices, coarse_cols, spacing, CB)
    windows = jnp.concatenate([rolled, jnp.roll(rolled, -1, axis=1)], axis=2)
    row_ids = (jnp.maximum(band_index - 1, 0), band_index, jnp.minimum(band_index + 1, rows_total - 1))
    weights_x = tent_x(spacing)
    summed = jnp.zeros((coarse_cols, realization_indices, 2 * spacing, CB), jnp.float32)
    for row_id, tent in zip(row_ids, tent_y(CB)):
        picked = lax.dynamic_index_in_dim(transforms, row_id, axis=1, keepdims=False)
        product = jnp.einsum('ckm,kcsy->cmsy', picked, windows, precision=precise)
        summed = summed + product * weights_x[:, None] * tent[None, :]
    cell_blocks = summed[:, :, :spacing] + jnp.roll(summed[:, :, spacing:], 1, axis=0)
    increment_step = cell_blocks.transpose(1, 0, 2, 3).reshape(realization_indices, coarse_cols * spacing, CB)
    return jnp.roll(increment_step, -(spacing // 2), axis=1)

def reference(background_samples, measured_space_anomalies, innovation_vector, error_spread_squared, measured_nearest_anchor, active_measurement_tally):
    realization_indices = background_samples.shape[0]
    background_centroid = lax.optimization_barrier(jnp.mean(background_samples, axis=0))
    sample_departure_matrix = background_samples - background_centroid[None]
    blocks = TX * TY * BANDS
    obs_blocks = measured_space_anomalies.reshape(realization_indices, TX, TY, BANDS, OBS_DEV).transpose(1, 2, 3, 0, 4).reshape(blocks, realization_indices, OBS_DEV)
    inputs = (obs_blocks, innovation_vector.reshape(blocks, OBS_DEV), error_spread_squared.reshape(blocks, OBS_DEV), measured_nearest_anchor.reshape(blocks, OBS_DEV), active_measurement_tally.reshape(blocks))
    transforms = lax.map(lambda values: transforms_block(*values), inputs)
    transforms = transforms.reshape(TX, TY, BANDS, CGX, realization_indices, realization_indices).transpose(0, 3, 1, 2, 4, 5)
    transforms = transforms.reshape(NCX, CROWS, realization_indices, realization_indices)
    deltas = lax.map(lambda band_index: band_delta(transforms, sample_departure_matrix, band_index), jnp.arange(CROWS, dtype=jnp.int32))
    increment_step = deltas.transpose(1, 2, 0, 3).reshape(realization_indices, LONGITUDE_CELLS, LATITUDE_CELLS)
    return background_centroid[None] + increment_step
```

```python
import math

import jax
import jax.numpy as jnp
from jax import lax
from jax.experimental import pallas as pl
from jax.experimental.pallas import tpu as pltpu
from jax.sharding import PartitionSpec as P

NS_PASSES = (3, 3, 3, 3, 2, 2)
MESH = pl.DeviceIdType.MESH
f32 = jnp.float32
bf16 = jnp.bfloat16
K = 256
NB = 8
MB = K // NB
SLOTS = 1024
CHUNKS = 4
CW = SLOTS // CHUNKS
LN = 128


def split(a, n):
    parts = []
    for i in range(n):
        part = a.astype(bf16)
        parts.append(part)
        if i < n - 1:
            a = a - part.astype(f32)
    return parts


def dot(a, b):
    return jnp.dot(a, b, preferred_element_type=f32)


def product(a, b):
    n = len(a)
    total = None
    for order in range(n - 1, -1, -1):
        for i in range(order, -1, -1):
            term = dot(a[i], b[order - i])
            total = term if total is None else total + term
    return total


def block_transpose(v):
    lane_block = lax.broadcasted_iota(jnp.int32, v[0].shape, 1) // 16
    for bit in (4, 2, 1):
        upper = (lane_block & bit) != 0
        new = list(v)
        for i in range(8):
            if i & bit == 0:
                a, b = v[i], v[i | bit]
                new[i] = jnp.where(upper, pltpu.roll(b, 16 * bit, 1), a)
                new[i | bit] = jnp.where(upper, b, pltpu.roll(a, LN - 16 * bit, 1))
        v = new
    return v


def column_of(g, xx):
    return (8 * g + 4 + xx) % 32


def kernel(
    bg, obs, dep, var, anchor, tally,
    out,
    bgs, outs, pk, yb, wts, cov, rhs, norm, y0, y1, y2, y3, z0, z1, z2, z3,
    pb, bh, bl, bh3, bl3, means, ts, tl, tr, cb, rb,
    bg_in, obs_send, obs_recv, bg_send, bg_recv, t_send, t_recv, c_send, c_recv,
):
    me = lax.axis_index("mem")
    gx = lax.axis_index("gx")
    gy = lax.axis_index("gy")
    gx_left, gx_right = lax.rem(gx + 7, 8), lax.rem(gx + 1, 8)
    gy_prev, gy_next = lax.rem(gy + 3, 4), lax.rem(gy + 1, 4)
    ys = (y0, y1, y2, y3)
    zs = (z0, z1, z2, z3)

    halves = [slice(0, LN), slice(LN, 2 * LN)]
    loads = [pltpu.make_async_copy(bg.at[:, halves[h]], bgs.at[h], bg_in.at[h]) for h in range(2)]
    for load in loads:
        load.start()

    barrier = pltpu.get_barrier_semaphore()

    def greet(**where):
        pl.semaphore_signal(barrier, inc=1, device_id=where, device_id_type=MESH)

    def each_peer(fn):
        def step(off, carry):
            fn(lax.rem(me + off, NB))
            return carry

        lax.fori_loop(1, NB, step, 0)

    def each_member(fn):
        def step(j, carry):
            fn(j)
            return carry

        lax.fori_loop(0, NB, step, 0)

    each_peer(lambda j: greet(mem=j))
    greet(gx=gx_left)
    greet(gx=gx_right)
    greet(mem=jnp.int32(0), gy=gy_next)
    greet(mem=jnp.int32(NB - 1), gy=gy_prev)

    @pl.when(me == 0)
    def _():
        each_member(lambda j: greet(mem=j, gy=gy_prev))

    @pl.when(me == NB - 1)
    def _():
        each_member(lambda j: greet(mem=j, gy=gy_next))

    mine = pl.ds(pl.multiple_of(me * MB, MB), MB)

    live = (lax.broadcasted_iota(jnp.int32, (1, SLOTS), 1) < tally[...]).astype(f32)
    for p in range(4):
        away = (anchor[...] - p).astype(f32)
        weight = jnp.exp(-0.5 * away * away) * live / var[...]
        wts[p : p + 1, :] = weight
        wts[p + 4 : p + 5, :] = weight * dep[...]

    pl.semaphore_wait(barrier, 11 + jnp.where((me == 0) | (me == NB - 1), NB, 0))

    def obs_copy(c, j):
        first = pl.multiple_of(j * SLOTS + c * CW, CW)
        return pltpu.make_async_remote_copy(
            src_ref=obs.at[:, pl.ds(first, CW)],
            dst_ref=yb.at[mine, pl.ds(c * CW, CW)],
            send_sem=obs_send,
            recv_sem=obs_recv.at[c],
            device_id={"mem": j},
            device_id_type=MESH,
        )

    for c in range(CHUNKS):
        first = pl.multiple_of(me * SLOTS + c * CW, CW)
        pltpu.make_async_copy(
            obs.at[:, pl.ds(first, CW)], yb.at[mine, pl.ds(c * CW, CW)], obs_recv.at[c]
        ).start()
        each_peer(lambda j: obs_copy(c, j).start())

    for load in loads:
        load.wait()
    for g in range(4):
        for half in range(2):
            v = [bgs[half, pl.ds(column_of(g, xx), MB, stride=32), :] for xx in range(8)]
            for i, w in enumerate(block_transpose(v)):
                pk[half * 8 + i, g] = w

    cov[...] = jnp.zeros_like(cov)
    rhs[...] = jnp.zeros_like(rhs)

    def cov_step(c, carry):
        lanes = pl.ds(pl.multiple_of(c * CW, CW), CW)
        here = yb.at[:, lanes]
        pltpu.make_async_copy(here, here, obs_recv.at[c]).wait()
        y = yb[:, lanes]
        yt = split(y.T, 3)
        for p in range(4):
            cov[p] += product(split(y * wts[p : p + 1, lanes], 3), yt)
        rhs[...] += product(split(wts[:, lanes], 3), yt)
        return carry

    lax.fori_loop(0, CHUNKS - 1, cov_step, 0)

    def bg_copies(b):
        def copy(src, dst, where):
            return pltpu.make_async_remote_copy(
                src_ref=src, dst_ref=dst, send_sem=bg_send, recv_sem=bg_recv,
                device_id=where, device_id_type=MESH,
            )

        to_next = lax.rem(gy + jnp.where(b == 0, 1, 0), 4)
        to_prev = lax.rem(gy + jnp.where(b == NB - 1, 3, 0), 4)
        below, above = lax.rem(2 * b + 15, 16), lax.rem(2 * b + 2, 16)
        return (
            lambda: copy(pk.at[pl.ds(2 * b, 2)], pb.at[pl.ds(1, 2), :, mine, :], {"mem": b}),
            lambda: copy(pk.at[below], pb.at[0, :, mine, :], {"mem": b, "gy": to_next}),
            lambda: copy(pk.at[above], pb.at[3, :, mine, :], {"mem": b, "gy": to_prev}),
        )

    def start_bg(b):
        for copy in bg_copies(b):
            copy().start()

    each_peer(start_bg)
    pltpu.make_async_copy(pk.at[pl.ds(2 * me, 2)], pb.at[pl.ds(1, 2), :, mine, :], bg_recv).start()
    for s, edge, which in ((0, 0, 1), (3, NB - 1, 2)):

        @pl.when(me == edge)
        def _():
            bg_copies(me)[which]().start()

        @pl.when(me != edge)
        def _():
            u = lax.rem(2 * me + (15 if s == 0 else 2), 16)
            pltpu.make_async_copy(pk.at[u], pb.at[s, :, mine, :], bg_recv).start()

    cov_step(jnp.int32(CHUNKS - 1), 0)

    row_id = lax.broadcasted_iota(jnp.int32, (K, K), 0)
    eye = (row_id == lax.broadcasted_iota(jnp.int32, (K, K), 1)).astype(f32)
    points = range(4)

    def two_steps(x, n):
        xs = [split(a, n) for a in x]
        xx = [product(a, a) for a in xs]
        us = [split(1.5 * x[p] - 0.5 * xx[p], n) for p in points]
        ms = [split(2.25 * eye - 1.5 * x[p] + 0.25 * xx[p], n) for p in points]
        v = [product(us[p], ms[p]) for p in points]
        return [2.25 * eye - 0.75 * x[p] - 0.5 * v[p] for p in points]

    def pair(n, last):
        zp = [split(z[...], n) for z in zs]
        yp = [split(y[...], n) for y in ys]
        w = two_steps([product(zp[p], yp[p]) for p in points], n)
        wp = [split(a, n) for a in w]
        for p in points:
            if not last:
                ys[p][...] = product(yp[p], wp[p])
            zs[p][...] = product(wp[p], zp[p])

    scaled = []
    for p in points:
        full = cov[p] + (K - 1.0) * eye
        size = jnp.sqrt(jnp.sum(full * full, axis=(0, 1), keepdims=True))
        norm[p : p + 1, :] = jnp.broadcast_to(size, (1, LN))
        scaled.append(full * (1.0 / size))
    w = two_steps(scaled, NS_PASSES[0])
    for p in points:
        ys[p][...] = product(split(scaled[p], NS_PASSES[0]), split(w[p], NS_PASSES[0]))
        zs[p][...] = w[p]
    exact = sum(1 for n in NS_PASSES[1:] if n == 3)
    lax.fori_loop(0, exact, lambda i, carry: (pair(3, False), carry)[1], 0)
    for k in range(1 + exact, 6):
        pair(NS_PASSES[k], k == 5)

    def finish(p):
        z = zs[p][...]
        size = norm[p : p + 1, 0:1]
        first = jnp.sum(z * rhs[p + 4 : p + 5, :], axis=1, keepdims=True)
        mean_weights = jnp.sum(z * first, axis=0, keepdims=True) / size
        ts[p] = z * (math.sqrt(K - 1.0) / jnp.sqrt(size)) + mean_weights

    def t_copy(p, dst, where, i):
        return pltpu.make_async_remote_copy(
            src_ref=ts.at[p], dst_ref=dst, send_sem=t_send.at[i], recv_sem=t_recv.at[i],
            device_id={"gx": where}, device_id_type=MESH,
        )

    to_left = t_copy(0, tr, gx_left, 0)
    to_right = t_copy(3, tl, gx_right, 1)
    finish(0)
    to_left.start()
    finish(3)
    to_right.start()
    finish(1)
    finish(2)

    pltpu.make_async_copy(pb, pb, bg_recv).wait()
    lane = lax.broadcasted_iota(jnp.int32, (1, LN), 1)
    xx = lane // 16
    weight_right = (xx.astype(f32) + 0.5) / 8.0
    weight_left = 1.0 - weight_right
    south_end = (me == 0) & (gy == 0)
    north_end = (me == NB - 1) & (gy == 3)
    for s in range(4):
        tent = 1.0 - jnp.abs((lane % 16).astype(f32) + (16 * s + 0.5 - 32.0)) / 32.0
        end = south_end if s < 2 else north_end
        tent = jnp.where(end, 0.0 if s in (0, 3) else 1.0, tent)
        cols = slice(s * LN, (s + 1) * LN)
        for g in range(4):
            slab = pb[s, g]
            mean = jnp.sum(slab, axis=0, keepdims=True) * (1.0 / K)
            means[4 * s + g : 4 * s + g + 1, :] = mean
            slab = slab - mean
            left, right = slab * (tent * weight_left), slab * (tent * weight_right)
            if g < 3:
                for i, part in enumerate((left, right)):
                    hi, lo = split(part, 2)
                    bh[g, i * K : (i + 1) * K, cols] = hi
                    bl[g, i * K : (i + 1) * K, cols] = lo
            else:
                east = xx < 4
                for i, part in enumerate((left, right)):
                    for k, kept in enumerate((east, jnp.logical_not(east))):
                        hi, lo = split(jnp.where(kept, part, 0.0), 2)
                        rows = slice((2 * k + i) * K, (2 * k + i + 1) * K)
                        bh3[rows, cols] = hi
                        bl3[rows, cols] = lo

    odd = lax.rem(me, 2)
    below, above = lax.rem(2 * me + 15, 16), lax.rem(2 * me + 2, 16)
    gy_below = lax.rem(gy + jnp.where(me == 0, 3, 0), 4)
    gy_above = lax.rem(gy + jnp.where(me == NB - 1, 1, 0), 4)

    def c_copies(g, j):
        rows = pl.ds(pl.multiple_of(j * MB, MB), MB)

        def copy(src, dst, where):
            return pltpu.make_async_remote_copy(
                src_ref=src, dst_ref=dst, send_sem=c_send, recv_sem=c_recv.at[g],
                device_id=where, device_id_type=MESH,
            )

        return (
            lambda: copy(cb.at[g, pl.ds(1, 2), rows, :], rb.at[g, odd, pl.ds(2 * me, 2)], {"mem": j}),
            lambda: copy(cb.at[g, 0, rows, :], rb.at[g, odd, below], {"mem": j, "gy": gy_below}),
            lambda: copy(cb.at[g, 3, rows, :], rb.at[g, odd, above], {"mem": j, "gy": gy_above}),
        )

    def start_c(g):
        def start(j):
            for copy in c_copies(g, j):
                copy().start()

        each_peer(start)
        pltpu.make_async_copy(
            cb.at[g, pl.ds(1, 2), mine, :], rb.at[g, odd, pl.ds(2 * me, 2)], c_recv.at[g]
        ).start()
        for s, edge, which, u in ((0, 0, 1, below), (3, NB - 1, 2, above)):

            @pl.when(me == edge)
            def _():
                c_copies(g, me)[which]().start()

            @pl.when(me != edge)
            def _():
                pltpu.make_async_copy(
                    cb.at[g, s, mine, :], rb.at[g, odd, u], c_recv.at[g]
                ).start()

    def shares(g, lhs, hi_ref, lo_ref):
        parts = [split(a, 2) for a in lhs]
        hi = jnp.concatenate([a[0] for a in parts], axis=1)
        lo = jnp.concatenate([a[1] for a in parts], axis=1)
        for pairs in range(2):
            cols = slice(2 * pairs * LN, 2 * (pairs + 1) * LN)
            b_hi, b_lo = hi_ref[:, cols], lo_ref[:, cols]
            total = (dot(lo, b_hi) + dot(hi, b_lo)) + dot(hi, b_hi)
            for i in range(2):
                s = 2 * pairs + i
                part = total[:, i * LN : (i + 1) * LN]
                if s in (1, 2):
                    part = part + means[4 * s + g : 4 * s + g + 1, :]
                cb[g, s] = part

    for g in range(3):
        shares(g, [ts[g], ts[g + 1]], bh.at[g], bl.at[g])
        start_c(g)
    to_left.wait_recv()
    to_right.wait_recv()
    shares(3, [ts[3], tr[...], tl[...], ts[0]], bh3, bl3)
    start_c(3)

    for g in range(4):
        pltpu.make_async_copy(rb.at[g], rb.at[g], c_recv.at[g]).wait()
        for half in range(2):
            v = [rb[g, 0, half * 8 + i] + rb[g, 1, half * 8 + i] for i in range(8)]
            for xx_, w in enumerate(block_transpose(v)):
                outs[half, pl.ds(column_of(g, xx_), MB, stride=32), :] = w
    stores = [pltpu.make_async_copy(outs.at[h], out.at[:, halves[h]], bg_in.at[h]) for h in range(2)]
    for store in stores:
        store.start()

    for store in stores:
        store.wait()

    to_left.wait_send()
    to_right.wait_send()
    most = yb.at[pl.ds(0, K - MB), :]
    pltpu.make_async_copy(most, most, obs_send).wait()
    most = pb.at[:, :, pl.ds(0, K - MB), :]
    pltpu.make_async_copy(most, most, bg_send).wait()
    most = cb.at[:, :, pl.ds(0, K - MB), :]
    pltpu.make_async_copy(most, most, c_send).wait()

    @pl.when((me == 0) | (me == NB - 1))
    def _():
        one = pb.at[0, :, pl.ds(0, MB), :]
        pltpu.make_async_copy(one, one, bg_send).wait()
        one = cb.at[:, 0, pl.ds(0, MB), :]
        pltpu.make_async_copy(one, one, c_send).wait()


def per_device(bg, obs, dep, var, anchor, tally):
    vmem = pl.BlockSpec(memory_space=pltpu.VMEM)
    anywhere = pl.BlockSpec(memory_space=pl.ANY)
    square = pltpu.VMEM((K, K), f32)
    dma = pltpu.SemaphoreType.DMA
    out = pl.pallas_call(
        kernel,
        out_shape=jax.ShapeDtypeStruct((MB * 32, 256), f32),
        in_specs=[anywhere, anywhere, vmem, vmem, vmem, vmem],
        out_specs=anywhere,
        scratch_shapes=[
            pltpu.VMEM((2, MB * 32, LN), f32),
            pltpu.VMEM((2, MB * 32, LN), f32),
            pltpu.VMEM((16, 4, MB, LN), f32),
            pltpu.VMEM((K, SLOTS), f32),
            pltpu.VMEM((8, SLOTS), f32),
            pltpu.VMEM((4, K, K), f32),
            pltpu.VMEM((8, K), f32),
            pltpu.VMEM((8, LN), f32),
            *[square] * 8,
            pltpu.VMEM((4, 4, K, LN), f32),
            pltpu.VMEM((3, 2 * K, 4 * LN), bf16),
            pltpu.VMEM((3, 2 * K, 4 * LN), bf16),
            pltpu.VMEM((4 * K, 4 * LN), bf16),
            pltpu.VMEM((4 * K, 4 * LN), bf16),
            pltpu.VMEM((16, LN), f32),
            pltpu.VMEM((4, K, K), f32),
            square,
            square,
            pltpu.VMEM((4, 4, K, LN), f32),
            pltpu.VMEM((4, 2, 16, MB, LN), f32),
            dma((2,)),
            dma,
            dma((CHUNKS,)),
            dma,
            dma,
            dma((2,)),
            dma((2,)),
            dma,
            dma((4,)),
        ],
        compiler_params=pltpu.CompilerParams(
            collective_id=0, has_side_effects=True, vmem_limit_bytes=48 << 20
        ),
        name="analysis",
    )(
        bg.reshape(MB * 32, 256),
        obs.reshape(MB, NB * SLOTS),
        dep.reshape(1, SLOTS),
        var.reshape(1, SLOTS),
        anchor.reshape(1, SLOTS),
        tally.reshape(1, 1),
    )
    return out.reshape(MB, 32, 256)


def solution(mesh):
    in_specs = (
        P("mem", "gx", "gy"),
        P("mem", "gx", "gy", None),
        P("gx", "gy", "mem", None),
        P("gx", "gy", "mem", None),
        P("gx", "gy", "mem", None),
        P("gx", "gy", "mem"),
    )
    return jax.shard_map(
        per_device, mesh=mesh, in_specs=in_specs, out_specs=P("mem", "gx", "gy"), check_vma=False
    )
```

```python
import math

import jax
import jax.numpy as jnp
from jax import lax
from jax.experimental import pallas as pl
from jax.experimental.pallas import tpu as pltpu
from jax.sharding import PartitionSpec as P

Y_PARTS = (3, 3, 3, 3, 2, 2)
MESH = pl.DeviceIdType.MESH
f32 = jnp.float32
bf16 = jnp.bfloat16
K = 256
NB = 8
MB = K // NB
SLOTS = 1024
CHUNKS = 4
CW = SLOTS // CHUNKS
LN = 128


def split(a, n):
    parts = []
    for i in range(n):
        part = a.astype(bf16)
        parts.append(part)
        if i < n - 1:
            a = a - part.astype(f32)
    return parts


def dot(a, b):
    return jnp.dot(a, b, preferred_element_type=f32)


def product(a, b):
    n = len(a)
    total = None
    for order in range(n - 1, -1, -1):
        for i in range(order, -1, -1):
            term = dot(a[i], b[order - i])
            total = term if total is None else total + term
    return total


def block_transpose(v):
    lane_block = lax.broadcasted_iota(jnp.int32, v[0].shape, 1) // 16
    for bit in (4, 2, 1):
        upper = (lane_block & bit) != 0
        new = list(v)
        for i in range(8):
            if i & bit == 0:
                a, b = v[i], v[i | bit]
                new[i] = jnp.where(upper, pltpu.roll(b, 16 * bit, 1), a)
                new[i | bit] = jnp.where(upper, b, pltpu.roll(a, LN - 16 * bit, 1))
        v = new
    return v


def column_of(g, xx):
    return (8 * g + 4 + xx) % 32


def kernel(
    bg, obs, dep, var, anchor, tally,
    out,
    bgs, pk, yb, wts, cov, rhs, norm, y0, y1, y2, y3, z0, z1, z2, z3,
    pb, bh, bl, bh3, bl3, means, ts, tl, tr, cb, rb,
    bg_in, obs_send, obs_recv, bg_send, bg_recv, t_send, t_recv, c_send, c_recv,
):
    me = lax.axis_index("mem")
    gx = lax.axis_index("gx")
    gy = lax.axis_index("gy")
    gx_left, gx_right = lax.rem(gx + 7, 8), lax.rem(gx + 1, 8)
    gy_prev, gy_next = lax.rem(gy + 3, 4), lax.rem(gy + 1, 4)
    ys = (y0, y1, y2, y3)
    zs = (z0, z1, z2, z3)

    halves = [slice(0, LN), slice(LN, 2 * LN)]
    loads = [pltpu.make_async_copy(bg.at[:, halves[h]], bgs.at[h], bg_in.at[h]) for h in range(2)]
    for load in loads:
        load.start()

    barrier = pltpu.get_barrier_semaphore()

    def greet(**where):
        pl.semaphore_signal(barrier, inc=1, device_id=where, device_id_type=MESH)

    def each_peer(fn):
        def step(off, carry):
            fn(lax.rem(me + off, NB))
            return carry

        lax.fori_loop(1, NB, step, 0)

    def each_member(fn):
        def step(j, carry):
            fn(j)
            return carry

        lax.fori_loop(0, NB, step, 0)

    each_peer(lambda j: greet(mem=j))
    greet(gx=gx_left)
    greet(gx=gx_right)
    greet(mem=jnp.int32(0), gy=gy_next)
    greet(mem=jnp.int32(NB - 1), gy=gy_prev)

    @pl.when(me == 0)
    def _():
        each_member(lambda j: greet(mem=j, gy=gy_prev))

    @pl.when(me == NB - 1)
    def _():
        each_member(lambda j: greet(mem=j, gy=gy_next))

    mine = pl.ds(pl.multiple_of(me * MB, MB), MB)

    live = (lax.broadcasted_iota(jnp.int32, (1, SLOTS), 1) < tally[...]).astype(f32)
    for p in range(4):
        away = (anchor[...] - p).astype(f32)
        weight = jnp.exp(-0.5 * away * away) * live / var[...]
        wts[p : p + 1, :] = weight
        wts[p + 4 : p + 5, :] = weight * dep[...]

    pl.semaphore_wait(barrier, 11 + jnp.where((me == 0) | (me == NB - 1), NB, 0))

    def obs_copy(c, j):
        first = pl.multiple_of(j * SLOTS + c * CW, CW)
        return pltpu.make_async_remote_copy(
            src_ref=obs.at[:, pl.ds(first, CW)],
            dst_ref=yb.at[mine, pl.ds(c * CW, CW)],
            send_sem=obs_send,
            recv_sem=obs_recv.at[c],
            device_id={"mem": j},
            device_id_type=MESH,
        )

    for c in range(CHUNKS):
        first = pl.multiple_of(me * SLOTS + c * CW, CW)
        pltpu.make_async_copy(
            obs.at[:, pl.ds(first, CW)], yb.at[mine, pl.ds(c * CW, CW)], obs_recv.at[c]
        ).start()
        each_peer(lambda j: obs_copy(c, j).start())

    for load in loads:
        load.wait()
    for g in range(4):
        for half in range(2):
            v = [bgs[half, pl.ds(column_of(g, xx), MB, stride=32), :] for xx in range(8)]
            for i, w in enumerate(block_transpose(v)):
                pk[half * 8 + i, g] = w

    cov[...] = jnp.zeros_like(cov)
    rhs[...] = jnp.zeros_like(rhs)

    def cov_step(c, carry):
        lanes = pl.ds(pl.multiple_of(c * CW, CW), CW)
        here = yb.at[:, lanes]
        pltpu.make_async_copy(here, here, obs_recv.at[c]).wait()
        y = yb[:, lanes]
        yt = split(y.T, 3)
        for p in range(4):
            cov[p] += product(split(y * wts[p : p + 1, lanes], 3), yt)
        rhs[...] += product(split(wts[:, lanes], 3), yt)
        return carry

    cov_step(jnp.int32(0), 0)

    def bg_start(g):
        def copy(src, dst, where):
            return pltpu.make_async_remote_copy(
                src_ref=src, dst_ref=dst, send_sem=bg_send, recv_sem=bg_recv.at[g],
                device_id=where, device_id_type=MESH,
            )

        def inner_copy(b):
            first = jnp.clip(2 * b - 1, 0, 12)
            return pk.at[pl.ds(first, 4), g], pb.at[:, g, mine, :]

        def middle_copy(b):
            return pk.at[pl.ds(2 * b, 2), g], pb.at[pl.ds(1, 2), g, mine, :]

        def side_copy(b, s):
            u = lax.rem(2 * b + (15 if s == 0 else 2), 16)
            return pk.at[u, g], pb.at[s, g, mine, :]

        def side_start(b, s):
            step = jnp.where(b == 0, 1, 0) if s == 0 else jnp.where(b == NB - 1, 3, 0)
            copy(*side_copy(b, s), {"mem": b, "gy": lax.rem(gy + step, 4)}).start()

        def start(b):
            within = (b > 0) & (b < NB - 1)

            @pl.when(within)
            def _():
                copy(*inner_copy(b), {"mem": b}).start()

            @pl.when(jnp.logical_not(within))
            def _():
                copy(*middle_copy(b), {"mem": b}).start()
                side_start(b, 0)
                side_start(b, 3)

        each_peer(start)
        pltpu.make_async_copy(*middle_copy(me), bg_recv.at[g]).start()
        for s, edge in ((0, 0), (3, NB - 1)):

            @pl.when(me == edge)
            def _():
                side_start(me, s)

            @pl.when(me != edge)
            def _():
                pltpu.make_async_copy(*side_copy(me, s), bg_recv.at[g]).start()

    for g in range(4):
        bg_start(g)

    lax.fori_loop(1, CHUNKS, cov_step, 0)

    row_id = lax.broadcasted_iota(jnp.int32, (K, K), 0)
    eye = (row_id == lax.broadcasted_iota(jnp.int32, (K, K), 1)).astype(f32)
    points = range(4)

    def two_steps(x, n):
        xs = [split(a, n) for a in x]
        xx = [product(a, a) for a in xs]
        us = [split(1.5 * x[p] - 0.5 * xx[p], n) for p in points]
        ms = [split(2.25 * eye - 1.5 * x[p] + 0.25 * xx[p], n) for p in points]
        v = [product(us[p], ms[p]) for p in points]
        return [2.25 * eye - 0.75 * x[p] - 0.5 * v[p] for p in points]

    def pair(n, last):
        zp = [split(z[...], 2) for z in zs]
        yp = [split(y[...], n) for y in ys]
        w = two_steps([product(zp[p], yp[p][:2]) for p in points], 2)
        wp = [split(a, n) for a in w]
        for p in points:
            if not last:
                ys[p][...] = product(yp[p], wp[p])
            zs[p][...] = product(wp[p][:2], zp[p])

    scaled = []
    for p in points:
        full = cov[p] + (K - 1.0) * eye
        size = jnp.sqrt(jnp.sum(full * full, axis=(0, 1), keepdims=True))
        norm[p : p + 1, :] = jnp.broadcast_to(size, (1, LN))
        scaled.append(full * (1.0 / size))
    w = two_steps(scaled, 2)
    for p in points:
        ys[p][...] = product(split(scaled[p], Y_PARTS[0]), split(w[p], Y_PARTS[0]))
        zs[p][...] = w[p]
    exact = sum(1 for n in Y_PARTS[1:] if n == 3)
    lax.fori_loop(0, exact, lambda i, carry: (pair(3, False), carry)[1], 0)
    for k in range(1 + exact, 6):
        pair(Y_PARTS[k], k == 5)

    def finish(p):
        z = zs[p][...]
        size = norm[p : p + 1, 0:1]
        first = jnp.sum(z * rhs[p + 4 : p + 5, :], axis=1, keepdims=True)
        mean_weights = jnp.sum(z * first, axis=0, keepdims=True) / size
        ts[p] = z * (math.sqrt(K - 1.0) / jnp.sqrt(size)) + mean_weights

    def t_copy(p, dst, where, i):
        return pltpu.make_async_remote_copy(
            src_ref=ts.at[p], dst_ref=dst, send_sem=t_send.at[i], recv_sem=t_recv.at[i],
            device_id={"gx": where}, device_id_type=MESH,
        )

    to_left = t_copy(0, tr, gx_left, 0)
    to_right = t_copy(3, tl, gx_right, 1)
    finish(0)
    to_left.start()
    finish(3)
    to_right.start()
    finish(1)

    lane = lax.broadcasted_iota(jnp.int32, (1, LN), 1)
    xx = lane // 16
    weight_right = (xx.astype(f32) + 0.5) / 8.0
    weight_left = 1.0 - weight_right
    south_end = (me == 0) & (gy == 0)
    north_end = (me == NB - 1) & (gy == 3)
    tents = []
    for s in range(4):
        tent = 1.0 - jnp.abs((lane % 16).astype(f32) + (16 * s + 0.5 - 32.0)) / 32.0
        end = south_end if s < 2 else north_end
        tents.append(jnp.where(end, 0.0 if s in (0, 3) else 1.0, tent))

    def prepare(g):
        here = pb.at[:, g]
        pltpu.make_async_copy(here, here, bg_recv.at[g]).wait()
        for s in range(4):
            cols = slice(s * LN, (s + 1) * LN)
            slab = pb[s, g]
            mean = jnp.sum(slab, axis=0, keepdims=True) * (1.0 / K)
            means[4 * s + g : 4 * s + g + 1, :] = mean
            slab = slab - mean
            left, right = slab * (tents[s] * weight_left), slab * (tents[s] * weight_right)
            if g < 3:
                for i, part in enumerate((left, right)):
                    hi, lo = split(part, 2)
                    bh[g, i * K : (i + 1) * K, cols] = hi
                    bl[g, i * K : (i + 1) * K, cols] = lo
            else:
                east = xx < 4
                for i, part in enumerate((left, right)):
                    for k, kept in enumerate((east, jnp.logical_not(east))):
                        hi, lo = split(jnp.where(kept, part, 0.0), 2)
                        rows = slice((2 * k + i) * K, (2 * k + i + 1) * K)
                        bh3[rows, cols] = hi
                        bl3[rows, cols] = lo

    odd = lax.rem(me, 2)
    below, above = lax.rem(2 * me + 15, 16), lax.rem(2 * me + 2, 16)
    gy_below = lax.rem(gy + jnp.where(me == 0, 3, 0), 4)
    gy_above = lax.rem(gy + jnp.where(me == NB - 1, 1, 0), 4)

    def c_copies(g, j):
        rows = pl.ds(pl.multiple_of(j * MB, MB), MB)

        def copy(src, dst, where):
            return pltpu.make_async_remote_copy(
                src_ref=src, dst_ref=dst, send_sem=c_send, recv_sem=c_recv.at[g],
                device_id=where, device_id_type=MESH,
            )

        return (
            lambda: copy(cb.at[g, pl.ds(1, 2), rows, :], rb.at[g, odd, pl.ds(2 * me, 2)], {"mem": j}),
            lambda: copy(cb.at[g, 0, rows, :], rb.at[g, odd, below], {"mem": j, "gy": gy_below}),
            lambda: copy(cb.at[g, 3, rows, :], rb.at[g, odd, above], {"mem": j, "gy": gy_above}),
        )

    inner = (me > 0) & (me < NB - 1)

    def c_whole(g, j):
        rows = pl.ds(pl.multiple_of(j * MB, MB), MB)
        first = jnp.clip(2 * me - 1, 0, 12)
        return pltpu.make_async_remote_copy(
            src_ref=cb.at[g, :, rows, :], dst_ref=rb.at[g, odd, pl.ds(first, 4)],
            send_sem=c_send, recv_sem=c_recv.at[g], device_id={"mem": j}, device_id_type=MESH,
        )

    def start_c(g):
        def start(j):
            @pl.when(inner)
            def _():
                c_whole(g, j).start()

            @pl.when(jnp.logical_not(inner))
            def _():
                for copy in c_copies(g, j):
                    copy().start()

        each_peer(start)
        pltpu.make_async_copy(
            cb.at[g, pl.ds(1, 2), mine, :], rb.at[g, odd, pl.ds(2 * me, 2)], c_recv.at[g]
        ).start()
        for s, edge, which, u in ((0, 0, 1, below), (3, NB - 1, 2, above)):

            @pl.when(me == edge)
            def _():
                c_copies(g, me)[which]().start()

            @pl.when(me != edge)
            def _():
                pltpu.make_async_copy(
                    cb.at[g, s, mine, :], rb.at[g, odd, u], c_recv.at[g]
                ).start()

    def shares(g, lhs, hi_ref, lo_ref):
        parts = [split(a, 2) for a in lhs]
        hi = jnp.concatenate([a[0] for a in parts], axis=1)
        lo = jnp.concatenate([a[1] for a in parts], axis=1)
        for pairs in range(2):
            cols = slice(2 * pairs * LN, 2 * (pairs + 1) * LN)
            b_hi, b_lo = hi_ref[:, cols], lo_ref[:, cols]
            total = (dot(lo, b_hi) + dot(hi, b_lo)) + dot(hi, b_hi)
            for i in range(2):
                s = 2 * pairs + i
                part = total[:, i * LN : (i + 1) * LN]
                if s in (1, 2):
                    part = part + means[4 * s + g : 4 * s + g + 1, :]
                cb[g, s] = part

    for g in range(3):
        if g == 1:
            finish(2)
        prepare(g)
        shares(g, [ts[g], ts[g + 1]], bh.at[g], bl.at[g])
        start_c(g)
    prepare(3)
    to_left.wait_recv()
    to_right.wait_recv()
    shares(3, [ts[3], tr[...], tl[...], ts[0]], bh3, bl3)
    start_c(3)

    for g in range(4):
        pltpu.make_async_copy(rb.at[g], rb.at[g], c_recv.at[g]).wait()
        for half in range(2):
            v = [rb[g, 0, half * 8 + i] + rb[g, 1, half * 8 + i] for i in range(8)]
            for xx_, w in enumerate(block_transpose(v)):
                out[half, pl.ds(column_of(g, xx_), MB, stride=32), :] = w

    to_left.wait_send()
    to_right.wait_send()
    most = yb.at[pl.ds(0, K - MB), :]
    pltpu.make_async_copy(most, most, obs_send).wait()
    most = pb.at[:, :, pl.ds(0, K - MB), :]
    pltpu.make_async_copy(most, most, bg_send).wait()
    most = cb.at[:, :, pl.ds(0, K - MB), :]
    pltpu.make_async_copy(most, most, c_send).wait()

    @pl.when((me == 0) | (me == NB - 1))
    def _():
        one = pb.at[0, :, pl.ds(0, MB), :]
        pltpu.make_async_copy(one, one, bg_send).wait()
        one = cb.at[:, 0, pl.ds(0, MB), :]
        pltpu.make_async_copy(one, one, c_send).wait()


def per_device(bg, obs, dep, var, anchor, tally):
    vmem = pl.BlockSpec(memory_space=pltpu.VMEM)
    anywhere = pl.BlockSpec(memory_space=pl.ANY)
    square = pltpu.VMEM((K, K), f32)
    dma = pltpu.SemaphoreType.DMA
    out = pl.pallas_call(
        kernel,
        out_shape=jax.ShapeDtypeStruct((2, MB * 32, LN), f32),
        in_specs=[anywhere, anywhere, vmem, vmem, vmem, vmem],
        out_specs=vmem,
        scratch_shapes=[
            pltpu.VMEM((2, MB * 32, LN), f32),
            pltpu.VMEM((16, 4, MB, LN), f32),
            pltpu.VMEM((K, SLOTS), f32),
            pltpu.VMEM((8, SLOTS), f32),
            pltpu.VMEM((4, K, K), f32),
            pltpu.VMEM((8, K), f32),
            pltpu.VMEM((8, LN), f32),
            *[square] * 8,
            pltpu.VMEM((4, 4, K, LN), f32),
            pltpu.VMEM((3, 2 * K, 4 * LN), bf16),
            pltpu.VMEM((3, 2 * K, 4 * LN), bf16),
            pltpu.VMEM((4 * K, 4 * LN), bf16),
            pltpu.VMEM((4 * K, 4 * LN), bf16),
            pltpu.VMEM((16, LN), f32),
            pltpu.VMEM((4, K, K), f32),
            square,
            square,
            pltpu.VMEM((4, 4, K, LN), f32),
            pltpu.VMEM((4, 2, 16, MB, LN), f32),
            dma((2,)),
            dma,
            dma((CHUNKS,)),
            dma,
            dma((4,)),
            dma((2,)),
            dma((2,)),
            dma,
            dma((4,)),
        ],
        compiler_params=pltpu.CompilerParams(
            collective_id=0, has_side_effects=True, vmem_limit_bytes=48 << 20
        ),
        name="analysis",
    )(
        bg.reshape(MB * 32, 256),
        obs.reshape(MB, NB * SLOTS),
        dep.reshape(1, SLOTS),
        var.reshape(1, SLOTS),
        anchor.reshape(1, SLOTS),
        tally.reshape(1, 1),
    )
    return out.reshape(2, MB, 32, LN).transpose(1, 2, 0, 3).reshape(MB, 32, 256)


def solution(mesh):
    in_specs = (
        P("mem", "gx", "gy"),
        P("mem", "gx", "gy", None),
        P("gx", "gy", "mem", None),
        P("gx", "gy", "mem", None),
        P("gx", "gy", "mem", None),
        P("gx", "gy", "mem"),
    )
    return jax.shard_map(
        per_device, mesh=mesh, in_specs=in_specs, out_specs=P("mem", "gx", "gy"), check_vma=False
    )
```

```python
import math

import jax
import jax.numpy as jnp
from jax import lax
from jax.experimental import pallas as pl
from jax.experimental.pallas import tpu as pltpu
from jax.sharding import PartitionSpec as P

Y_PARTS = (3, 3, 3, 3, 2, 2)
MESH = pl.DeviceIdType.MESH
f32 = jnp.float32
bf16 = jnp.bfloat16
K = 256
NB = 8
MB = K // NB
SLOTS = 1024
CHUNKS = 4
CW = SLOTS // CHUNKS
LN = 128


def split(a, n):
    parts = []
    for i in range(n):
        part = a.astype(bf16)
        parts.append(part)
        if i < n - 1:
            a = a - part.astype(f32)
    return parts


def dot(a, b):
    return jnp.dot(a, b, preferred_element_type=f32)


def product(a, b):
    n = len(a)
    total = None
    for order in range(n - 1, -1, -1):
        for i in range(order, -1, -1):
            term = dot(a[i], b[order - i])
            total = term if total is None else total + term
    return total


def block_transpose(v):
    lane_block = lax.broadcasted_iota(jnp.int32, v[0].shape, 1) // 16
    for bit in (4, 2, 1):
        upper = (lane_block & bit) != 0
        new = list(v)
        for i in range(8):
            if i & bit == 0:
                a, b = v[i], v[i | bit]
                new[i] = jnp.where(upper, pltpu.roll(b, 16 * bit, 1), a)
                new[i | bit] = jnp.where(upper, b, pltpu.roll(a, LN - 16 * bit, 1))
        v = new
    return v


def column_of(g, xx):
    return (8 * g + 4 + xx) % 32


def kernel(
    bg, obs, dep, var, anchor, tally,
    out,
    bgs, pk, yb, wts, cov, rhs, norm, y0, y1, y2, y3, z0, z1, z2, z3,
    pb, bh, bl, bh3, bl3, means, ts, tl, tr, cb, rb,
    bg_in, obs_send, obs_recv, bg_send, bg_recv, t_send, t_recv, c_send, c_recv,
):
    me = lax.axis_index("mem")
    gx = lax.axis_index("gx")
    gy = lax.axis_index("gy")
    gx_left, gx_right = lax.rem(gx + 7, 8), lax.rem(gx + 1, 8)
    gy_prev, gy_next = lax.rem(gy + 3, 4), lax.rem(gy + 1, 4)
    ys = (y0, y1, y2, y3)
    zs = (z0, z1, z2, z3)

    halves = [slice(0, LN), slice(LN, 2 * LN)]
    loads = [pltpu.make_async_copy(bg.at[:, halves[h]], bgs.at[h], bg_in.at[h]) for h in range(2)]
    for load in loads:
        load.start()

    barrier = pltpu.get_barrier_semaphore()

    def greet(**where):
        pl.semaphore_signal(barrier, inc=1, device_id=where, device_id_type=MESH)

    def each_peer(fn):
        def step(off, carry):
            fn(lax.rem(me + off, NB))
            return carry

        lax.fori_loop(1, NB, step, 0)

    each_peer(lambda j: greet(mem=j))
    greet(gx=gx_left)
    greet(gx=gx_right)
    greet(gy=gy_prev)
    greet(gy=gy_next)

    mine = pl.ds(pl.multiple_of(me * MB, MB), MB)

    live = (lax.broadcasted_iota(jnp.int32, (1, SLOTS), 1) < tally[...]).astype(f32)
    for p in range(4):
        away = (anchor[...] - p).astype(f32)
        weight = jnp.exp(-0.5 * away * away) * live / var[...]
        wts[p : p + 1, :] = weight
        wts[p + 4 : p + 5, :] = weight * dep[...]

    pl.semaphore_wait(barrier, NB + 3)

    def obs_copy(c, j):
        first = pl.multiple_of(j * SLOTS + c * CW, CW)
        return pltpu.make_async_remote_copy(
            src_ref=obs.at[:, pl.ds(first, CW)],
            dst_ref=yb.at[mine, pl.ds(c * CW, CW)],
            send_sem=obs_send,
            recv_sem=obs_recv.at[c],
            device_id={"mem": j},
            device_id_type=MESH,
        )

    for c in range(CHUNKS):
        first = pl.multiple_of(me * SLOTS + c * CW, CW)
        pltpu.make_async_copy(
            obs.at[:, pl.ds(first, CW)], yb.at[mine, pl.ds(c * CW, CW)], obs_recv.at[c]
        ).start()
        each_peer(lambda j: obs_copy(c, j).start())

    for load in loads:
        load.wait()
    for g in range(4):
        for half in range(2):
            v = [bgs[half, pl.ds(column_of(g, xx), MB, stride=32), :] for xx in range(8)]
            for i, w in enumerate(block_transpose(v)):
                pk[half * 8 + i, g] = w

    cov[...] = jnp.zeros_like(cov)
    rhs[...] = jnp.zeros_like(rhs)

    def cov_step(c, carry):
        lanes = pl.ds(pl.multiple_of(c * CW, CW), CW)
        here = yb.at[:, lanes]
        pltpu.make_async_copy(here, here, obs_recv.at[c]).wait()
        y = yb[:, lanes]
        yt = split(y.T, 3)
        for p in range(4):
            cov[p] += product(split(y * wts[p : p + 1, lanes], 3), yt)
        rhs[...] += product(split(wts[:, lanes], 3), yt)
        return carry

    cov_step(jnp.int32(0), 0)

    def bg_start(g):
        def copy(src, dst, where):
            return pltpu.make_async_remote_copy(
                src_ref=src, dst_ref=dst, send_sem=bg_send, recv_sem=bg_recv.at[g],
                device_id=where, device_id_type=MESH,
            )

        def inner_copy(b):
            first = jnp.clip(2 * b - 1, 0, 12)
            return pk.at[pl.ds(first, 4), g], pb.at[:, g, mine, :]

        def middle_copy(b):
            return pk.at[pl.ds(2 * b, 2), g], pb.at[pl.ds(1, 2), g, mine, :]

        def side_copy(b, s):
            u = lax.rem(2 * b + (15 if s == 0 else 2), 16)
            return pk.at[u, g], pb.at[s, g, mine, :]

        def side_start(b, s):
            step = jnp.where(b == 0, 1, 0) if s == 0 else jnp.where(b == NB - 1, 3, 0)
            copy(*side_copy(b, s), {"mem": b, "gy": lax.rem(gy + step, 4)}).start()

        def start(b):
            within = (b > 0) & (b < NB - 1)

            @pl.when(within)
            def _():
                copy(*inner_copy(b), {"mem": b}).start()

            @pl.when(jnp.logical_not(within))
            def _():
                copy(*middle_copy(b), {"mem": b}).start()
                side_start(b, 0)
                side_start(b, 3)

        each_peer(start)
        pltpu.make_async_copy(*middle_copy(me), bg_recv.at[g]).start()
        for s, edge in ((0, 0), (3, NB - 1)):

            @pl.when(me == edge)
            def _():
                side_start(me, s)

            @pl.when(me != edge)
            def _():
                pltpu.make_async_copy(*side_copy(me, s), bg_recv.at[g]).start()

    for g in range(4):
        bg_start(g)

    lax.fori_loop(1, CHUNKS, cov_step, 0)

    row_id = lax.broadcasted_iota(jnp.int32, (K, K), 0)
    eye = (row_id == lax.broadcasted_iota(jnp.int32, (K, K), 1)).astype(f32)
    points = range(4)

    def two_steps(x, n):
        xs = [split(a, n) for a in x]
        xx = [product(a, a) for a in xs]
        us = [split(1.5 * x[p] - 0.5 * xx[p], n) for p in points]
        ms = [split(2.25 * eye - 1.5 * x[p] + 0.25 * xx[p], n) for p in points]
        v = [product(us[p], ms[p]) for p in points]
        return [2.25 * eye - 0.75 * x[p] - 0.5 * v[p] for p in points]

    def pair(n, last):
        zp = [split(z[...], 2) for z in zs]
        yp = [split(y[...], n) for y in ys]
        w = two_steps([product(zp[p], yp[p][:2]) for p in points], 2)
        wp = [split(a, n) for a in w]
        for p in points:
            if not last:
                ys[p][...] = product(yp[p], wp[p])
            zs[p][...] = product(wp[p][:2], zp[p])

    scaled = []
    for p in points:
        full = cov[p] + (K - 1.0) * eye
        size = jnp.sqrt(jnp.sum(full * full, axis=(0, 1), keepdims=True))
        norm[p : p + 1, :] = jnp.broadcast_to(size, (1, LN))
        scaled.append(full * (1.0 / size))
    w = two_steps(scaled, 2)
    for p in points:
        ys[p][...] = product(split(scaled[p], Y_PARTS[0]), split(w[p], Y_PARTS[0]))
        zs[p][...] = w[p]
    exact = sum(1 for n in Y_PARTS[1:] if n == 3)
    lax.fori_loop(0, exact, lambda i, carry: (pair(3, False), carry)[1], 0)
    for k in range(1 + exact, 6):
        pair(Y_PARTS[k], k == 5)

    def finish(p):
        z = zs[p][...]
        size = norm[p : p + 1, 0:1]
        first = jnp.sum(z * rhs[p + 4 : p + 5, :], axis=1, keepdims=True)
        mean_weights = jnp.sum(z * first, axis=0, keepdims=True) / size
        ts[p] = z * (math.sqrt(K - 1.0) / jnp.sqrt(size)) + mean_weights

    def t_copy(p, dst, where, i):
        return pltpu.make_async_remote_copy(
            src_ref=ts.at[p], dst_ref=dst, send_sem=t_send.at[i], recv_sem=t_recv.at[i],
            device_id={"gx": where}, device_id_type=MESH,
        )

    to_left = t_copy(0, tr, gx_left, 0)
    to_right = t_copy(3, tl, gx_right, 1)
    finish(0)
    to_left.start()
    finish(3)
    to_right.start()
    finish(1)

    lane = lax.broadcasted_iota(jnp.int32, (1, LN), 1)
    xx = lane // 16
    weight_right = (xx.astype(f32) + 0.5) / 8.0
    weight_left = 1.0 - weight_right
    south_end = (me == 0) & (gy == 0)
    north_end = (me == NB - 1) & (gy == 3)
    tents = []
    for s in range(4):
        tent = 1.0 - jnp.abs((lane % 16).astype(f32) + (16 * s + 0.5 - 32.0)) / 32.0
        end = south_end if s < 2 else north_end
        tents.append(jnp.where(end, 0.0 if s in (0, 3) else 1.0, tent))

    def prepare(g):
        here = pb.at[:, g]
        pltpu.make_async_copy(here, here, bg_recv.at[g]).wait()
        for s in range(4):
            cols = slice(s * LN, (s + 1) * LN)
            slab = pb[s, g]
            mean = jnp.sum(slab, axis=0, keepdims=True) * (1.0 / K)
            means[4 * s + g : 4 * s + g + 1, :] = mean
            slab = slab - mean
            left, right = slab * (tents[s] * weight_left), slab * (tents[s] * weight_right)
            if g < 3:
                for i, part in enumerate((left, right)):
                    hi, lo = split(part, 2)
                    bh[g, i * K : (i + 1) * K, cols] = hi
                    bl[g, i * K : (i + 1) * K, cols] = lo
            else:
                east = xx < 4
                for i, part in enumerate((left, right)):
                    for k, kept in enumerate((east, jnp.logical_not(east))):
                        hi, lo = split(jnp.where(kept, part, 0.0), 2)
                        rows = slice((2 * k + i) * K, (2 * k + i + 1) * K)
                        bh3[rows, cols] = hi
                        bl3[rows, cols] = lo

    odd = lax.rem(me, 2)
    below, above = lax.rem(2 * me + 15, 16), lax.rem(2 * me + 2, 16)
    gy_below = lax.rem(gy + jnp.where(me == 0, 3, 0), 4)
    gy_above = lax.rem(gy + jnp.where(me == NB - 1, 1, 0), 4)

    def c_copies(g, j):
        rows = pl.ds(pl.multiple_of(j * MB, MB), MB)

        def copy(src, dst, where):
            return pltpu.make_async_remote_copy(
                src_ref=src, dst_ref=dst, send_sem=c_send, recv_sem=c_recv.at[g],
                device_id=where, device_id_type=MESH,
            )

        return (
            lambda: copy(cb.at[g, pl.ds(1, 2), rows, :], rb.at[g, odd, pl.ds(2 * me, 2)], {"mem": j}),
            lambda: copy(cb.at[g, 0, rows, :], rb.at[g, odd, below], {"mem": j, "gy": gy_below}),
            lambda: copy(cb.at[g, 3, rows, :], rb.at[g, odd, above], {"mem": j, "gy": gy_above}),
        )

    inner = (me > 0) & (me < NB - 1)

    def c_whole(g, j):
        rows = pl.ds(pl.multiple_of(j * MB, MB), MB)
        first = jnp.clip(2 * me - 1, 0, 12)
        return pltpu.make_async_remote_copy(
            src_ref=cb.at[g, :, rows, :], dst_ref=rb.at[g, odd, pl.ds(first, 4)],
            send_sem=c_send, recv_sem=c_recv.at[g], device_id={"mem": j}, device_id_type=MESH,
        )

    def start_c(g):
        def start(j):
            @pl.when(inner)
            def _():
                c_whole(g, j).start()

            @pl.when(jnp.logical_not(inner))
            def _():
                for copy in c_copies(g, j):
                    copy().start()

        each_peer(start)
        pltpu.make_async_copy(
            cb.at[g, pl.ds(1, 2), mine, :], rb.at[g, odd, pl.ds(2 * me, 2)], c_recv.at[g]
        ).start()
        for s, edge, which, u in ((0, 0, 1, below), (3, NB - 1, 2, above)):

            @pl.when(me == edge)
            def _():
                c_copies(g, me)[which]().start()

            @pl.when(me != edge)
            def _():
                pltpu.make_async_copy(
                    cb.at[g, s, mine, :], rb.at[g, odd, u], c_recv.at[g]
                ).start()

    def shares(g, lhs, hi_ref, lo_ref):
        parts = [split(a, 2) for a in lhs]
        hi = jnp.concatenate([a[0] for a in parts], axis=1)
        lo = jnp.concatenate([a[1] for a in parts], axis=1)
        for pairs in range(2):
            cols = slice(2 * pairs * LN, 2 * (pairs + 1) * LN)
            b_hi, b_lo = hi_ref[:, cols], lo_ref[:, cols]
            total = (dot(lo, b_hi) + dot(hi, b_lo)) + dot(hi, b_hi)
            for i in range(2):
                s = 2 * pairs + i
                part = total[:, i * LN : (i + 1) * LN]
                if s in (1, 2):
                    part = part + means[4 * s + g : 4 * s + g + 1, :]
                cb[g, s] = part

    for g in range(3):
        if g == 1:
            finish(2)
        prepare(g)
        shares(g, [ts[g], ts[g + 1]], bh.at[g], bl.at[g])
        start_c(g)
    prepare(3)
    to_left.wait_recv()
    to_right.wait_recv()
    shares(3, [ts[3], tr[...], tl[...], ts[0]], bh3, bl3)
    start_c(3)

    for g in range(4):
        pltpu.make_async_copy(rb.at[g], rb.at[g], c_recv.at[g]).wait()
        for half in range(2):
            v = [rb[g, 0, half * 8 + i] + rb[g, 1, half * 8 + i] for i in range(8)]
            for xx_, w in enumerate(block_transpose(v)):
                out[half, pl.ds(column_of(g, xx_), MB, stride=32), :] = w

    to_left.wait_send()
    to_right.wait_send()
    most = yb.at[pl.ds(0, K - MB), :]
    pltpu.make_async_copy(most, most, obs_send).wait()
    most = pb.at[:, :, pl.ds(0, K - MB), :]
    pltpu.make_async_copy(most, most, bg_send).wait()
    most = cb.at[:, :, pl.ds(0, K - MB), :]
    pltpu.make_async_copy(most, most, c_send).wait()

    @pl.when((me == 0) | (me == NB - 1))
    def _():
        one = pb.at[0, :, pl.ds(0, MB), :]
        pltpu.make_async_copy(one, one, bg_send).wait()
        one = cb.at[:, 0, pl.ds(0, MB), :]
        pltpu.make_async_copy(one, one, c_send).wait()


def per_device(bg, obs, dep, var, anchor, tally):
    vmem = pl.BlockSpec(memory_space=pltpu.VMEM)
    anywhere = pl.BlockSpec(memory_space=pl.ANY)
    square = pltpu.VMEM((K, K), f32)
    dma = pltpu.SemaphoreType.DMA
    out = pl.pallas_call(
        kernel,
        out_shape=jax.ShapeDtypeStruct((2, MB * 32, LN), f32),
        in_specs=[anywhere, anywhere, vmem, vmem, vmem, vmem],
        out_specs=vmem,
        scratch_shapes=[
            pltpu.VMEM((2, MB * 32, LN), f32),
            pltpu.VMEM((16, 4, MB, LN), f32),
            pltpu.VMEM((K, SLOTS), f32),
            pltpu.VMEM((8, SLOTS), f32),
            pltpu.VMEM((4, K, K), f32),
            pltpu.VMEM((8, K), f32),
            pltpu.VMEM((8, LN), f32),
            *[square] * 8,
            pltpu.VMEM((4, 4, K, LN), f32),
            pltpu.VMEM((3, 2 * K, 4 * LN), bf16),
            pltpu.VMEM((3, 2 * K, 4 * LN), bf16),
            pltpu.VMEM((4 * K, 4 * LN), bf16),
            pltpu.VMEM((4 * K, 4 * LN), bf16),
            pltpu.VMEM((16, LN), f32),
            pltpu.VMEM((4, K, K), f32),
            square,
            square,
            pltpu.VMEM((4, 4, K, LN), f32),
            pltpu.VMEM((4, 2, 16, MB, LN), f32),
            dma((2,)),
            dma,
            dma((CHUNKS,)),
            dma,
            dma((4,)),
            dma((2,)),
            dma((2,)),
            dma,
            dma((4,)),
        ],
        compiler_params=pltpu.CompilerParams(
            collective_id=0, has_side_effects=True, vmem_limit_bytes=48 << 20
        ),
        name="analysis",
    )(
        bg.reshape(MB * 32, 256),
        obs.reshape(MB, NB * SLOTS),
        dep.reshape(1, SLOTS),
        var.reshape(1, SLOTS),
        anchor.reshape(1, SLOTS),
        tally.reshape(1, 1),
    )
    return out.reshape(2, MB, 32, LN).transpose(1, 2, 0, 3).reshape(MB, 32, 256)


def solution(mesh):
    in_specs = (
        P("mem", "gx", "gy"),
        P("mem", "gx", "gy", None),
        P("gx", "gy", "mem", None),
        P("gx", "gy", "mem", None),
        P("gx", "gy", "mem", None),
        P("gx", "gy", "mem"),
    )
    return jax.shard_map(
        per_device, mesh=mesh, in_specs=in_specs, out_specs=P("mem", "gx", "gy"), check_vma=False
    )
```

```python
import math

import jax
import jax.numpy as jnp
from jax import lax
from jax.experimental import pallas as pl
from jax.experimental.pallas import tpu as pltpu
from jax.sharding import PartitionSpec as P

Y_PARTS = (3, 3, 3, 3, 2, 2)
MESH = pl.DeviceIdType.MESH
f32 = jnp.float32
bf16 = jnp.bfloat16
K = 256
NB = 8
MB = K // NB
SLOTS = 1024
CHUNKS = 4
CW = SLOTS // CHUNKS
LN = 128


def split(a, n):
    parts = []
    for i in range(n):
        part = a.astype(bf16)
        parts.append(part)
        if i < n - 1:
            a = a - part.astype(f32)
    return parts


def dot(a, b):
    return jnp.dot(a, b, preferred_element_type=f32)


def product(a, b):
    n = len(a)
    total = None
    for order in range(n - 1, -1, -1):
        for i in range(order, -1, -1):
            term = dot(a[i], b[order - i])
            total = term if total is None else total + term
    return total


def block_transpose(v):
    lane_block = lax.broadcasted_iota(jnp.int32, v[0].shape, 1) // 16
    for bit in (4, 2, 1):
        upper = (lane_block & bit) != 0
        new = list(v)
        for i in range(8):
            if i & bit == 0:
                a, b = v[i], v[i | bit]
                new[i] = jnp.where(upper, pltpu.roll(b, 16 * bit, 1), a)
                new[i | bit] = jnp.where(upper, b, pltpu.roll(a, LN - 16 * bit, 1))
        v = new
    return v


def column_of(g, xx):
    return (8 * g + 4 + xx) % 32


def kernel(
    bg, obs, dep, var, anchor, tally,
    out,
    bgs, pk, yb, wts, cov, rhs, norm, y0, y1, y2, y3, z0, z1, z2, z3,
    pb, bh, bl, bh3, bl3, means, ts, tl, tr, cb, rb,
    bg_in, obs_send, obs_recv, bg_send, bg_recv, t_send, t_recv, c_send, c_recv,
):
    me = lax.axis_index("mem")
    gx = lax.axis_index("gx")
    gy = lax.axis_index("gy")
    gx_left, gx_right = lax.rem(gx + 7, 8), lax.rem(gx + 1, 8)
    gy_prev, gy_next = lax.rem(gy + 3, 4), lax.rem(gy + 1, 4)
    ys = (y0, y1, y2, y3)
    zs = (z0, z1, z2, z3)

    halves = [slice(0, LN), slice(LN, 2 * LN)]
    loads = [pltpu.make_async_copy(bg.at[:, halves[h]], bgs.at[h], bg_in.at[h]) for h in range(2)]
    barrier = pltpu.get_barrier_semaphore()

    def greet(**where):
        pl.semaphore_signal(barrier, inc=1, device_id=where, device_id_type=MESH)

    def each_peer(fn):
        def step(off, carry):
            fn(lax.rem(me + off, NB))
            return carry

        lax.fori_loop(1, NB, step, 0)

    greet(gy=gy_prev)
    greet(gy=gy_next)
    greet(gx=gx_left)
    greet(gx=gx_right)
    each_peer(lambda j: greet(mem=j))

    for load in loads:
        load.start()

    mine = pl.ds(pl.multiple_of(me * MB, MB), MB)

    live = (lax.broadcasted_iota(jnp.int32, (1, SLOTS), 1) < tally[...]).astype(f32)
    for p in range(4):
        away = (anchor[...] - p).astype(f32)
        weight = jnp.exp(-0.5 * away * away) * live / var[...]
        wts[p : p + 1, :] = weight
        wts[p + 4 : p + 5, :] = weight * dep[...]

    pl.semaphore_wait(barrier, NB + 3)

    def obs_copy(c, j):
        first = pl.multiple_of(j * SLOTS + c * CW, CW)
        return pltpu.make_async_remote_copy(
            src_ref=obs.at[:, pl.ds(first, CW)],
            dst_ref=yb.at[mine, pl.ds(c * CW, CW)],
            send_sem=obs_send,
            recv_sem=obs_recv.at[c],
            device_id={"mem": j},
            device_id_type=MESH,
        )

    for c in range(CHUNKS):
        first = pl.multiple_of(me * SLOTS + c * CW, CW)
        pltpu.make_async_copy(
            obs.at[:, pl.ds(first, CW)], yb.at[mine, pl.ds(c * CW, CW)], obs_recv.at[c]
        ).start()
        each_peer(lambda j: obs_copy(c, j).start())

    for load in loads:
        load.wait()
    for g in range(4):
        for half in range(2):
            v = [bgs[half, pl.ds(column_of(g, xx), MB, stride=32), :] for xx in range(8)]
            for i, w in enumerate(block_transpose(v)):
                pk[half * 8 + i, g] = w

    cov[...] = jnp.zeros_like(cov)
    rhs[...] = jnp.zeros_like(rhs)

    def cov_step(c, carry):
        lanes = pl.ds(pl.multiple_of(c * CW, CW), CW)
        here = yb.at[:, lanes]
        pltpu.make_async_copy(here, here, obs_recv.at[c]).wait()
        y = yb[:, lanes]
        yt = split(y.T, 3)
        for p in range(4):
            cov[p] += product(split(y * wts[p : p + 1, lanes], 3), yt)
        rhs[...] += product(split(wts[:, lanes], 3), yt)
        return carry

    cov_step(jnp.int32(0), 0)

    def bg_start(g):
        def copy(src, dst, where):
            return pltpu.make_async_remote_copy(
                src_ref=src, dst_ref=dst, send_sem=bg_send, recv_sem=bg_recv.at[g],
                device_id=where, device_id_type=MESH,
            )

        def inner_copy(b):
            first = jnp.clip(2 * b - 1, 0, 12)
            return pk.at[pl.ds(first, 4), g], pb.at[:, g, mine, :]

        def middle_copy(b):
            return pk.at[pl.ds(2 * b, 2), g], pb.at[pl.ds(1, 2), g, mine, :]

        def side_copy(b, s):
            u = lax.rem(2 * b + (15 if s == 0 else 2), 16)
            return pk.at[u, g], pb.at[s, g, mine, :]

        def side_start(b, s):
            step = jnp.where(b == 0, 1, 0) if s == 0 else jnp.where(b == NB - 1, 3, 0)
            copy(*side_copy(b, s), {"mem": b, "gy": lax.rem(gy + step, 4)}).start()

        def start(b):
            within = (b > 0) & (b < NB - 1)

            @pl.when(within)
            def _():
                copy(*inner_copy(b), {"mem": b}).start()

            @pl.when(jnp.logical_not(within))
            def _():
                copy(*middle_copy(b), {"mem": b}).start()
                side_start(b, 0)
                side_start(b, 3)

        each_peer(start)
        pltpu.make_async_copy(*middle_copy(me), bg_recv.at[g]).start()
        for s, edge in ((0, 0), (3, NB - 1)):

            @pl.when(me == edge)
            def _():
                side_start(me, s)

            @pl.when(me != edge)
            def _():
                pltpu.make_async_copy(*side_copy(me, s), bg_recv.at[g]).start()

    for g in range(4):
        bg_start(g)

    lax.fori_loop(1, CHUNKS, cov_step, 0)

    row_id = lax.broadcasted_iota(jnp.int32, (K, K), 0)
    eye = (row_id == lax.broadcasted_iota(jnp.int32, (K, K), 1)).astype(f32)
    points = range(4)

    def two_steps(x, n):
        xs = [split(a, n) for a in x]
        xx = [product(a, a) for a in xs]
        us = [split(1.5 * x[p] - 0.5 * xx[p], n) for p in points]
        ms = [split(2.25 * eye - 1.5 * x[p] + 0.25 * xx[p], n) for p in points]
        v = [product(us[p], ms[p]) for p in points]
        return [2.25 * eye - 0.75 * x[p] - 0.5 * v[p] for p in points]

    def pair(n, last):
        zp = [split(z[...], 2) for z in zs]
        yp = [split(y[...], n) for y in ys]
        w = two_steps([product(zp[p], yp[p][:2]) for p in points], 2)
        wp = [split(a, n) for a in w]
        for p in points:
            if not last:
                ys[p][...] = product(yp[p], wp[p])
            zs[p][...] = product(wp[p][:2], zp[p])

    scaled = []
    for p in points:
        full = cov[p] + (K - 1.0) * eye
        size = jnp.sqrt(jnp.sum(full * full, axis=(0, 1), keepdims=True))
        norm[p : p + 1, :] = jnp.broadcast_to(size, (1, LN))
        scaled.append(full * (1.0 / size))
    w = two_steps(scaled, 2)
    for p in points:
        ys[p][...] = product(split(scaled[p], Y_PARTS[0]), split(w[p], Y_PARTS[0]))
        zs[p][...] = w[p]
    exact = sum(1 for n in Y_PARTS[1:] if n == 3)
    lax.fori_loop(0, exact, lambda i, carry: (pair(3, False), carry)[1], 0)
    for k in range(1 + exact, 6):
        pair(Y_PARTS[k], k == 5)

    def finish(p):
        z = zs[p][...]
        size = norm[p : p + 1, 0:1]
        first = jnp.sum(z * rhs[p + 4 : p + 5, :], axis=1, keepdims=True)
        mean_weights = jnp.sum(z * first, axis=0, keepdims=True) / size
        ts[p] = z * (math.sqrt(K - 1.0) / jnp.sqrt(size)) + mean_weights

    def t_copy(p, dst, where, i):
        return pltpu.make_async_remote_copy(
            src_ref=ts.at[p], dst_ref=dst, send_sem=t_send.at[i], recv_sem=t_recv.at[i],
            device_id={"gx": where}, device_id_type=MESH,
        )

    to_left = t_copy(0, tr, gx_left, 0)
    to_right = t_copy(3, tl, gx_right, 1)
    finish(0)
    to_left.start()
    finish(3)
    to_right.start()
    finish(1)

    lane = lax.broadcasted_iota(jnp.int32, (1, LN), 1)
    xx = lane // 16
    weight_right = (xx.astype(f32) + 0.5) / 8.0
    weight_left = 1.0 - weight_right
    south_end = (me == 0) & (gy == 0)
    north_end = (me == NB - 1) & (gy == 3)
    tents = []
    for s in range(4):
        tent = 1.0 - jnp.abs((lane % 16).astype(f32) + (16 * s + 0.5 - 32.0)) / 32.0
        end = south_end if s < 2 else north_end
        tents.append(jnp.where(end, 0.0 if s in (0, 3) else 1.0, tent))

    def prepare(g):
        here = pb.at[:, g]
        pltpu.make_async_copy(here, here, bg_recv.at[g]).wait()
        for s in range(4):
            cols = slice(s * LN, (s + 1) * LN)
            slab = pb[s, g]
            mean = jnp.sum(slab, axis=0, keepdims=True) * (1.0 / K)
            means[4 * s + g : 4 * s + g + 1, :] = mean
            slab = slab - mean
            left, right = slab * (tents[s] * weight_left), slab * (tents[s] * weight_right)
            if g < 3:
                for i, part in enumerate((left, right)):
                    hi, lo = split(part, 2)
                    bh[g, i * K : (i + 1) * K, cols] = hi
                    bl[g, i * K : (i + 1) * K, cols] = lo
            else:
                east = xx < 4
                for i, part in enumerate((left, right)):
                    for k, kept in enumerate((east, jnp.logical_not(east))):
                        hi, lo = split(jnp.where(kept, part, 0.0), 2)
                        rows = slice((2 * k + i) * K, (2 * k + i + 1) * K)
                        bh3[rows, cols] = hi
                        bl3[rows, cols] = lo

    odd = lax.rem(me, 2)
    below, above = lax.rem(2 * me + 15, 16), lax.rem(2 * me + 2, 16)
    gy_below = lax.rem(gy + jnp.where(me == 0, 3, 0), 4)
    gy_above = lax.rem(gy + jnp.where(me == NB - 1, 1, 0), 4)

    def c_copies(g, j):
        rows = pl.ds(pl.multiple_of(j * MB, MB), MB)

        def copy(src, dst, where):
            return pltpu.make_async_remote_copy(
                src_ref=src, dst_ref=dst, send_sem=c_send, recv_sem=c_recv.at[g],
                device_id=where, device_id_type=MESH,
            )

        return (
            lambda: copy(cb.at[g, pl.ds(1, 2), rows, :], rb.at[g, odd, pl.ds(2 * me, 2)], {"mem": j}),
            lambda: copy(cb.at[g, 0, rows, :], rb.at[g, odd, below], {"mem": j, "gy": gy_below}),
            lambda: copy(cb.at[g, 3, rows, :], rb.at[g, odd, above], {"mem": j, "gy": gy_above}),
        )

    inner = (me > 0) & (me < NB - 1)

    def c_whole(g, j):
        rows = pl.ds(pl.multiple_of(j * MB, MB), MB)
        first = jnp.clip(2 * me - 1, 0, 12)
        return pltpu.make_async_remote_copy(
            src_ref=cb.at[g, :, rows, :], dst_ref=rb.at[g, odd, pl.ds(first, 4)],
            send_sem=c_send, recv_sem=c_recv.at[g], device_id={"mem": j}, device_id_type=MESH,
        )

    def start_c(g):
        def start(j):
            @pl.when(inner)
            def _():
                c_whole(g, j).start()

            @pl.when(jnp.logical_not(inner))
            def _():
                for copy in c_copies(g, j):
                    copy().start()

        each_peer(start)
        pltpu.make_async_copy(
            cb.at[g, pl.ds(1, 2), mine, :], rb.at[g, odd, pl.ds(2 * me, 2)], c_recv.at[g]
        ).start()
        for s, edge, which, u in ((0, 0, 1, below), (3, NB - 1, 2, above)):

            @pl.when(me == edge)
            def _():
                c_copies(g, me)[which]().start()

            @pl.when(me != edge)
            def _():
                pltpu.make_async_copy(
                    cb.at[g, s, mine, :], rb.at[g, odd, u], c_recv.at[g]
                ).start()

    def shares(g, lhs, hi_ref, lo_ref):
        parts = [split(a, 2) for a in lhs]
        hi = jnp.concatenate([a[0] for a in parts], axis=1)
        lo = jnp.concatenate([a[1] for a in parts], axis=1)
        for pairs in range(2):
            cols = slice(2 * pairs * LN, 2 * (pairs + 1) * LN)
            b_hi, b_lo = hi_ref[:, cols], lo_ref[:, cols]
            total = (dot(lo, b_hi) + dot(hi, b_lo)) + dot(hi, b_hi)
            for i in range(2):
                s = 2 * pairs + i
                part = total[:, i * LN : (i + 1) * LN]
                if s in (1, 2):
                    part = part + means[4 * s + g : 4 * s + g + 1, :]
                cb[g, s] = part

    for g in range(3):
        if g == 1:
            finish(2)
        prepare(g)
        shares(g, [ts[g], ts[g + 1]], bh.at[g], bl.at[g])
        start_c(g)
    prepare(3)
    to_left.wait_recv()
    to_right.wait_recv()
    shares(3, [ts[3], tr[...], tl[...], ts[0]], bh3, bl3)
    start_c(3)

    for g in range(4):
        pltpu.make_async_copy(rb.at[g], rb.at[g], c_recv.at[g]).wait()
        for half in range(2):
            v = [rb[g, 0, half * 8 + i] + rb[g, 1, half * 8 + i] for i in range(8)]
            for xx_, w in enumerate(block_transpose(v)):
                out[half, pl.ds(column_of(g, xx_), MB, stride=32), :] = w

    to_left.wait_send()
    to_right.wait_send()
    most = yb.at[pl.ds(0, K - MB), :]
    pltpu.make_async_copy(most, most, obs_send).wait()
    most = pb.at[:, :, pl.ds(0, K - MB), :]
    pltpu.make_async_copy(most, most, bg_send).wait()
    most = cb.at[:, :, pl.ds(0, K - MB), :]
    pltpu.make_async_copy(most, most, c_send).wait()

    @pl.when((me == 0) | (me == NB - 1))
    def _():
        one = pb.at[0, :, pl.ds(0, MB), :]
        pltpu.make_async_copy(one, one, bg_send).wait()
        one = cb.at[:, 0, pl.ds(0, MB), :]
        pltpu.make_async_copy(one, one, c_send).wait()


def per_device(bg, obs, dep, var, anchor, tally):
    vmem = pl.BlockSpec(memory_space=pltpu.VMEM)
    anywhere = pl.BlockSpec(memory_space=pl.ANY)
    square = pltpu.VMEM((K, K), f32)
    dma = pltpu.SemaphoreType.DMA
    out = pl.pallas_call(
        kernel,
        out_shape=jax.ShapeDtypeStruct((2, MB * 32, LN), f32),
        in_specs=[anywhere, anywhere, vmem, vmem, vmem, vmem],
        out_specs=vmem,
        scratch_shapes=[
            pltpu.VMEM((2, MB * 32, LN), f32),
            pltpu.VMEM((16, 4, MB, LN), f32),
            pltpu.VMEM((K, SLOTS), f32),
            pltpu.VMEM((8, SLOTS), f32),
            pltpu.VMEM((4, K, K), f32),
            pltpu.VMEM((8, K), f32),
            pltpu.VMEM((8, LN), f32),
            *[square] * 8,
            pltpu.VMEM((4, 4, K, LN), f32),
            pltpu.VMEM((3, 2 * K, 4 * LN), bf16),
            pltpu.VMEM((3, 2 * K, 4 * LN), bf16),
            pltpu.VMEM((4 * K, 4 * LN), bf16),
            pltpu.VMEM((4 * K, 4 * LN), bf16),
            pltpu.VMEM((16, LN), f32),
            pltpu.VMEM((4, K, K), f32),
            square,
            square,
            pltpu.VMEM((4, 4, K, LN), f32),
            pltpu.VMEM((4, 2, 16, MB, LN), f32),
            dma((2,)),
            dma,
            dma((CHUNKS,)),
            dma,
            dma((4,)),
            dma((2,)),
            dma((2,)),
            dma,
            dma((4,)),
        ],
        compiler_params=pltpu.CompilerParams(
            collective_id=0, has_side_effects=True, vmem_limit_bytes=48 << 20
        ),
        name="analysis",
    )(
        bg.reshape(MB * 32, 256),
        obs.reshape(MB, NB * SLOTS),
        dep.reshape(1, SLOTS),
        var.reshape(1, SLOTS),
        anchor.reshape(1, SLOTS),
        tally.reshape(1, 1),
    )
    return out.reshape(2, MB, 32, LN).transpose(1, 2, 0, 3).reshape(MB, 32, 256)


def solution(mesh):
    in_specs = (
        P("mem", "gx", "gy"),
        P("mem", "gx", "gy", None),
        P("gx", "gy", "mem", None),
        P("gx", "gy", "mem", None),
        P("gx", "gy", "mem", None),
        P("gx", "gy", "mem"),
    )
    return jax.shard_map(
        per_device, mesh=mesh, in_specs=in_specs, out_specs=P("mem", "gx", "gy"), check_vma=False
    )
```
